128 devices in a mesh: pair: 32 (over x, y, core), grid: 4 (over z).
Axes of the slice: x: 4, y: 4, z: 4, core: 2. Of those that a mesh axis runs over, the one named last changes fastest.
Arguments:
- b_tiles: float32 [8192, 128, 128], P(('pair', 'grid')), may hold values from -0.6 to 0.6
- tile_aux: int32 [8192], P(('pair', 'grid')), may hold values from 0 to 19, as said below
- tile_pair: int32 [8192], P(('pair', 'grid')), may hold values from 0 to 1535, as said below
- freq_weights: float32 [2, 196608], P(None, ('pair', 'grid')), may hold values from 0.1 to 2
- kept: int32 [128, 2], replicated, may hold values from 0 to 19, as said below
Outputs:
- pi_tiles: float32 [128, 2, 128, 128], P(('pair', 'grid'))
The draws below stay inside these ranges and needn't reach their ends.
Inputs may be any that keep to these rules, and one draw needn't show every extreme that they name: `tile_aux`: never falling along the list. `tile_pair`: pair block b belongs to the device at index b // 12 of pair+grid. Of the tiles on one device at most 2 belong to one device's pair blocks, and in every draw some device receives exactly 2 tiles from every device. `kept`: each row (P, Q) has P < Q, and no two rows are equal.
All inputs are finite; a program needn't handle non-finite values.
Results may differ from the reference program's by a relative error of at most 0.00012.
Values sent between devices are 32-bit elements; how exact they have to be, the bound alone decides.
No kernel may reach another device: no remote copies, remote signals or barrier semaphores. Data moves between devices by JAX's collectives and lax.ppermute only.
A program may use at most 256 MiB of HBM per device.

```python
import math
import jax
import jax.numpy as jnp
import numpy as np
from jax import lax

TILE = 128
NAB = 20
PB_DEV = 12
BT_DEV = 64
CAP = 2
NBT = 8192
NPB = 1536
NPAIRS = 196608
NPT = 128
DEVICES = 128


def draw_tile_aux(key, part):
    key = jax.random.fold_in(key, 11)
    values = jax.random.randint(key, (BT_DEV * DEVICES,), 0, NAB)
    return jnp.sort(values).astype(jnp.int32)


def draw_tile_pair(key, part):
    key = jax.random.fold_in(key, 23)
    hot_key, rest_key = jax.random.split(key)
    hottest = jax.random.randint(hot_key, (), 0, DEVICES)

    def one_source(source_key):
        order_key, local_key, mix_key = jax.random.split(source_key, 3)
        others = jnp.arange(CAP * (DEVICES - 1), dtype=jnp.int32) // CAP
        others = others + (others >= hottest).astype(jnp.int32)
        chosen = jax.random.permutation(order_key, others)[:BT_DEV - CAP]
        owners = jnp.concatenate([jnp.full((CAP,), hottest, jnp.int32), chosen.astype(jnp.int32)])
        owners = jax.random.permutation(mix_key, owners)
        local_block = jax.random.randint(local_key, (BT_DEV,), 0, PB_DEV)
        return owners * PB_DEV + local_block
    source_keys = jax.random.split(rest_key, DEVICES)
    return jax.vmap(one_source)(source_keys).reshape(-1).astype(jnp.int32)


def draw_kept(key, part):
    key = jax.random.fold_in(key, 37)
    first_rows, second_rows = np.triu_indices(NAB, 1)
    order = jax.random.permutation(key, first_rows.shape[0])[:NPT]
    first_block = jnp.asarray(first_rows, dtype=jnp.int32)[order]
    second_block = jnp.asarray(second_rows, dtype=jnp.int32)[order]
    return jnp.stack([first_block, second_block], axis=1).astype(jnp.int32)


def block_scale(rng, shape, cuts, least, top_value):
    factor_of = 1.0
    for dim, blocks in cuts:
        draws = jax.random.uniform(jax.random.fold_in(jax.random.fold_in(rng, 6), dim), (blocks,), jnp.float32, least / len(cuts), top_value / len(cuts))
        factor_of = factor_of * jnp.repeat(jnp.exp(draws), shape[dim] // blocks).reshape((-1,) + (1,) * (len(shape) - 1 - dim))
    return factor_of


def scatter_about(rng, dims, width, reach, pieces=(), kind=jnp.bfloat16):
    values = jax.random.normal(rng, dims, jnp.float32) * width
    if len(pieces) > 0:
        values = block_scale(rng, dims, pieces, -0.22, 0.18) * values
    return jnp.clip(values, min=-reach, max=reach).astype(kind)


def setup_inputs(seed: int = 0) -> dict:
    keys = jax.random.split(jax.random.key(seed), 6)
    return {
        "b_tiles": scatter_about(keys[0], (NBT, TILE, TILE), 0.1, 0.6, ((0, 128),), jnp.float32),
        "tile_aux": draw_tile_aux(jax.random.fold_in(keys[5], 71), 0),
        "tile_pair": draw_tile_pair(jax.random.fold_in(keys[5], 71), 0),
        "freq_weights": jnp.clip(jnp.exp(math.log(2.0) - 2.9957323 * jax.random.uniform(keys[3], (2, NPAIRS), jnp.float32) ** block_scale(keys[3], (2, NPAIRS), ((1, 128),), -0.2, 0.2)), 0.1, 2.0),
        "kept": draw_kept(jax.random.fold_in(keys[5], 71), 0),
    }


def reference(b_tiles, tile_aux, tile_pair, freq_weights, kept):
    dense_b = jnp.zeros((NAB, NPB, TILE, TILE), jnp.float32).at[tile_aux, tile_pair].add(b_tiles)
    weights = freq_weights.reshape(2, NPB, TILE)

    def one_tile(pair_ids):
        left_rows = dense_b[pair_ids[0]]
        right_rows = dense_b[pair_ids[1]]
        scaled = left_rows[None] * weights[:, :, None, :]
        return jnp.einsum("fnik,njk->fij", scaled, right_rows, precision=lax.Precision.HIGHEST)

    return lax.map(one_tile, kept)
```

```python
import functools

import jax
import jax.numpy as jnp
from jax import lax
from jax.experimental import pallas as pl
from jax.experimental.pallas import tpu as pltpu
from jax.sharding import Mesh
from jax.sharding import PartitionSpec as P

NAB = 20
T = 128
FREQS = 2
EXTRA = 8
ALL = ("x", "y", "core", "z")
CHIPS = ("x", "y", "z")
NT = (((1,), (1,)), ((), ()))
MIB = 1024 * 1024


def columns_kernel(groups, tiles_ref, keys_ref, weights_ref, out_ref):
    step = pl.program_id(0)
    flat = out_ref.reshape(T * 8, T)

    @pl.when(step < groups)
    def _():
        for k in range(8):
            flat[pl.ds(k, T, stride=8), :] = tiles_ref[k].T

    @pl.when(step == groups)
    def _():
        out_ref[...] = jnp.zeros_like(out_ref)
        flat[pl.ds(0, T, stride=8), :] = jnp.broadcast_to(keys_ref[...], (T, T))
        flat[pl.ds(1, T, stride=8), :] = weights_ref[...].T


def by_column(b_tiles, keys, weights):
    count = b_tiles.shape[0]
    groups = count // 8
    out = pl.pallas_call(
        functools.partial(columns_kernel, groups),
        grid=(groups + 1,),
        in_specs=[
            pl.BlockSpec((8, T, T), lambda g: (jnp.minimum(g, groups - 1), 0, 0)),
            pl.BlockSpec((1, T), lambda g: (0, 0)),
            pl.BlockSpec((T, T), lambda g: (0, 0)),
        ],
        out_specs=pl.BlockSpec((T, None, 8, T), lambda g: (0, g, 0, 0)),
        out_shape=jax.ShapeDtypeStruct((T, groups + 1, 8, T), jnp.float32),
        name="columns",
    )(b_tiles, keys, weights)
    return out


def expand_kernel(count, blocks, got_ref, bt_ref, w_ref, rows, keys, starts, acc):
    pairs = blocks * T
    chunks = rows.shape[0] - 1
    a = pl.program_id(0)

    @pl.when(a == 0)
    def _():
        per = T // count

        def fill(s, carry):
            x = got_ref[pl.ds(per * s, per), 0:count, :].reshape(T, T).T
            hi = x.astype(jnp.bfloat16)
            rows[s, 0:T, :] = hi
            rows[s, T:, :] = (x - hi.astype(jnp.float32)).astype(jnp.bfloat16)
            key = jnp.sum(got_ref[pl.ds(per * s, per), count, :], axis=0, keepdims=True)
            keys[pl.ds(s, 1), :] = key.astype(jnp.int32)
            return carry

        lax.fori_loop(0, chunks, fill, 0)
        rows[chunks] = jnp.zeros_like(rows[chunks])
        keys[pl.ds(chunks, 8), :] = jnp.full((8, T), -1, jnp.int32)
        w_ref[...] = got_ref[:, count + 1, :].T
        held = keys[0:chunks, :]
        for i in range(NAB + 1):
            starts[i] = jnp.sum((held < i * pairs).astype(jnp.int32))

    first = starts[a]
    last = starts[a + 1]
    base = first // T
    steps = jnp.where(last > first, (last - base * T + 2 * T - 1) // (2 * T), 0)
    acc[...] = jnp.zeros_like(acc)
    place = lax.broadcasted_iota(jnp.int32, (2 * T, 2 * T), 0)

    def add(j, carry):
        s = base + 2 * j
        left = jnp.concatenate([rows[s], rows[s + 1]], axis=1)
        key = jnp.concatenate([keys[pl.ds(s, 1), :], keys[pl.ds(s + 1, 1), :]], axis=1) - a * pairs
        for n in range(pairs // (2 * T)):
            hot = jnp.where(place == key - n * 2 * T, 1.0, 0.0).astype(jnp.bfloat16)
            acc[:, n * 2 * T : (n + 1) * 2 * T] += lax.dot_general(
                left, hot, NT, preferred_element_type=jnp.float32
            )
        return carry

    lax.fori_loop(0, steps, add, 0)
    total = acc[0:T, :] + acc[T:, :]
    hi = total.astype(jnp.bfloat16)
    bt_ref[0:T, :] = hi
    bt_ref[T:, :] = (total - hi.astype(jnp.float32)).astype(jnp.bfloat16)


def expand(got, count, blocks):
    sources = got.shape[0]
    chunks = sources * count // T
    pairs = blocks * T
    return pl.pallas_call(
        functools.partial(expand_kernel, count, blocks),
        grid=(NAB,),
        in_specs=[pl.BlockSpec(memory_space=pltpu.VMEM)],
        out_specs=[
            pl.BlockSpec((None, 2 * T, pairs), lambda a: (a, 0, 0)),
            pl.BlockSpec((T, T), lambda a: (0, 0)),
        ],
        out_shape=[
            jax.ShapeDtypeStruct((NAB, 2 * T, pairs), jnp.bfloat16),
            jax.ShapeDtypeStruct((T, T), jnp.float32),
        ],
        scratch_shapes=[
            pltpu.VMEM((chunks + 1, 2 * T, T), jnp.bfloat16),
            pltpu.VMEM((chunks + 8, T), jnp.int32),
            pltpu.SMEM((NAB + 1,), jnp.int32),
            pltpu.VMEM((2 * T, pairs), jnp.float32),
        ],
        compiler_params=pltpu.CompilerParams(vmem_limit_bytes=40 * MIB),
        name="expand",
    )(got)


def tiles_kernel(blocks, picks, bt_ref, w_ref, out_ref, right_hi, right_lo, first, row_of, slot_of, stage, sems):
    count = picks.shape[0] // 2
    for q in range(NAB + 1):
        first[q] = 0

    def tally(t, carry):
        q = picks[2 * t + 1]
        first[q] = first[q] + 1
        return carry

    lax.fori_loop(0, count, tally, 0)
    total = jnp.int32(0)
    for q in range(NAB + 1):
        here = first[q]
        first[q] = total
        total = total + here

    def arrange(t, carry):
        q = picks[2 * t + 1]
        at = first[q]
        first[q] = at + 1
        row_of[at] = picks[2 * t]
        slot_of[at] = t
        return carry

    lax.fori_loop(0, count, arrange, 0)

    def column(q, begin):
        end = first[q]

        @pl.when(end > begin)
        def _():
            for n in range(blocks):
                lanes = slice(n * T, (n + 1) * T)
                whole = bt_ref[q, 0:T, lanes].astype(jnp.float32) + bt_ref[q, T:, lanes].astype(jnp.float32)
                for f in range(FREQS):
                    scaled = whole * w_ref[f * blocks + n : f * blocks + n + 1, :]
                    hi = scaled.astype(jnp.bfloat16)
                    right_hi[f * T : (f + 1) * T, lanes] = hi
                    right_lo[f * T : (f + 1) * T, lanes] = (scaled - hi.astype(jnp.float32)).astype(jnp.bfloat16)

        def tile(at, carry):
            p = row_of[at]
            t = slot_of[at]
            both = lax.dot_general(bt_ref[p], right_hi[...], NT, preferred_element_type=jnp.float32)
            small = lax.dot_general(bt_ref[p, 0:T, :], right_lo[...], NT, preferred_element_type=jnp.float32)
            result = both[0:T] + (both[T:] + small)
            for f in range(FREQS):
                stage[t, f] = result[:, f * T : (f + 1) * T]
            pltpu.make_async_copy(stage.at[t], out_ref.at[t], sems.at[0]).start()
            return carry

        lax.fori_loop(begin, end, tile, 0)
        return end

    lax.fori_loop(0, NAB, column, jnp.int32(0))
    pltpu.make_async_copy(stage, out_ref, sems.at[0]).wait()


def tiles(picks, bt, w, blocks):
    count = picks.shape[0]
    pairs = blocks * T
    return pl.pallas_call(
        functools.partial(tiles_kernel, blocks),
        grid_spec=pltpu.PrefetchScalarGridSpec(
            num_scalar_prefetch=1,
            grid=(),
            in_specs=[pl.BlockSpec(memory_space=pltpu.VMEM)] * 2,
            out_specs=pl.BlockSpec(memory_space=pl.ANY),
            scratch_shapes=[
                pltpu.VMEM((FREQS * T, pairs), jnp.bfloat16),
                pltpu.VMEM((FREQS * T, pairs), jnp.bfloat16),
                pltpu.SMEM((NAB + 1,), jnp.int32),
                pltpu.SMEM((count,), jnp.int32),
                pltpu.SMEM((count,), jnp.int32),
                pltpu.VMEM((count, FREQS, T, T), jnp.float32),
                pltpu.SemaphoreType.DMA((1,)),
            ],
        ),
        out_shape=jax.ShapeDtypeStruct((count, FREQS, T, T), jnp.float32),
        compiler_params=pltpu.CompilerParams(vmem_limit_bytes=44 * MIB),
        cost_estimate=pl.CostEstimate(
            flops=6 * count * FREQS * T * T * pairs, bytes_accessed=20 * MIB, transcendentals=0
        ),
        name="tiles",
    )(picks.reshape(-1), bt, w)


def on_device(b_tiles, tile_aux, tile_pair, freq_weights, kept):
    count = b_tiles.shape[0]
    devices = lax.axis_size(ALL)
    chips = lax.axis_size(CHIPS)
    me = lax.axis_index(ALL)
    core = lax.axis_index("core")
    blocks = freq_weights.shape[1] // T

    key = tile_aux * (blocks * devices) + (tile_pair % blocks) * devices + tile_pair // blocks
    per = T // count
    lane = jnp.arange(T, dtype=jnp.int32)
    keys = jnp.where(lane // count == me % per, jnp.tile(key, per), 0).astype(jnp.float32)[None]
    weights = jnp.pad(freq_weights.reshape(FREQS * blocks, T), ((0, T - FREQS * blocks), (0, 0)))
    sent = by_column(b_tiles, keys, weights).reshape(devices, count + EXTRA, T)
    got = lax.all_to_all(sent, ALL, split_axis=0, concat_axis=0, tiled=True)

    bt, w = expand(got, count, blocks)
    picks = kept.reshape(lax.axis_size("x") * lax.axis_size("y"), 2, lax.axis_size("z"), 2)
    mine = lax.dynamic_index_in_dim(picks, core, 1, keepdims=False).reshape(chips, 2)
    other = lax.dynamic_index_in_dim(picks, 1 - core, 1, keepdims=False).reshape(chips, 2)
    away = tiles(other, bt, w, blocks)
    landed = lax.ppermute(away, "core", [(0, 1), (1, 0)])
    own = tiles(mine, bt, w, blocks)
    both = own + landed
    parts = lax.all_to_all(both, CHIPS, split_axis=0, concat_axis=0, tiled=True)
    return jnp.sum(parts, axis=0, keepdims=True)


def solution(mesh):
    fine = Mesh(mesh.devices.reshape(4, 4, 2, 4), ALL)
    placed = (P(ALL, None, None), P(ALL), P(ALL), P(None, ALL), P())
    return jax.shard_map(
        on_device, mesh=fine, in_specs=placed, out_specs=P(ALL, None, None, None), check_vma=False
    )
```

```python
import functools

import jax
import jax.numpy as jnp
from jax import lax
from jax.experimental import pallas as pl
from jax.experimental.pallas import tpu as pltpu
from jax.sharding import Mesh
from jax.sharding import PartitionSpec as P

NAB = 20
T = 128
FREQS = 2
EXTRA = 8
FIRST = 4
MIB = 1024 * 1024
GROUP = 4
AHEAD = 8
BF16 = jnp.bfloat16
F32 = jnp.float32


def columns_kernel(groups, blocks, devices, tiles_ref, aux_ref, pair_ref, weights_ref, out_ref):
    step = pl.program_id(0)
    flat = out_ref.reshape(T * 8, T)

    @pl.when(step < groups)
    def _():
        for k in range(8):
            flat[pl.ds(k, T, stride=8), :] = tiles_ref[k].T

    @pl.when(step == groups)
    def _():
        out_ref[...] = jnp.zeros_like(out_ref)
        pair = pair_ref[...].astype(F32)
        source = jnp.floor((pair + 0.5) * (1.0 / blocks))
        key = aux_ref[...].astype(F32) * (blocks * devices) + (pair - source * blocks) * devices + source
        key = jnp.concatenate([key] * (T // key.shape[1]), axis=1)
        flat[pl.ds(0, T, stride=8), :] = jnp.broadcast_to(key, (T, T))
        rows = [weights_ref[f : f + 1, n * T : (n + 1) * T] for f in range(FREQS) for n in range(blocks)]
        rows.append(jnp.zeros((T - FREQS * blocks, T), F32))
        flat[pl.ds(1, T, stride=8), :] = jnp.concatenate(rows, axis=0).T


def by_column(b_tiles, aux, pair, weights, devices):
    count = b_tiles.shape[0]
    groups = count // 8
    blocks = weights.shape[1] // T
    return pl.pallas_call(
        functools.partial(columns_kernel, groups, blocks, devices),
        grid=(groups + 1,),
        in_specs=[
            pl.BlockSpec((8, T, T), lambda g: (jnp.minimum(g, groups - 1), 0, 0)),
            pl.BlockSpec((1, count), lambda g: (0, 0)),
            pl.BlockSpec((1, count), lambda g: (0, 0)),
            pl.BlockSpec(weights.shape, lambda g: (0, 0)),
        ],
        out_specs=pl.BlockSpec((T, None, 8, T), lambda g: (0, g, 0, 0)),
        out_shape=jax.ShapeDtypeStruct((T, groups + 1, 8, T), F32),
        name="columns",
    )(b_tiles, aux[None], pair[None], weights)


def sort_picks(picks, count, first, row_of, column_of, slot_of):
    for q in range(NAB):
        first[q] = 0

    def tally(t, carry):
        q = picks[2 * t + 1]
        first[q] = first[q] + 1
        return carry

    lax.fori_loop(0, count, tally, 0)
    total = jnp.int32(0)
    for q in range(NAB):
        here = first[q]
        first[q] = total
        total = total + here

    def arrange(t, carry):
        q = picks[2 * t + 1]
        at = first[q]
        first[q] = at + 1
        row_of[at] = picks[2 * t]
        column_of[at] = q
        slot_of[at] = t
        return carry

    lax.fori_loop(0, count, arrange, 0)


def multiply(lists, left, right, stage, outs, out_sems, ready):
    row_of, column_of, slot_of = lists
    count = row_of.shape[0]
    share = count // len(outs)

    def group(g, reached):
        reached = ready(reached, column_of[g * GROUP + GROUP - 1] + 1)
        buffer = lax.rem(g, 2)
        done = pltpu.make_async_copy(stage.at[buffer], outs[0].at[pl.ds(0, GROUP)], out_sems.at[buffer])

        @pl.when(g >= 2)
        def _():
            done.wait()

        for k in range(GROUP):
            at = g * GROUP + k
            p = row_of[at]
            q = column_of[at] - 1
            both = jnp.dot(left[p], right[q, 0], preferred_element_type=F32)
            small = jnp.dot(left[p, 0:T, :], right[q, 1], preferred_element_type=F32)
            result = both[0:T] + (both[T:] + small)
            for f in range(FREQS):
                stage[buffer, k, f] = result[:, f * T : (f + 1) * T]
        for k in range(GROUP):
            t = slot_of[g * GROUP + k]
            for i, out in enumerate(outs):

                @pl.when(t // share == i)
                def _():
                    pltpu.make_async_copy(
                        stage.at[buffer, k], out.at[t - i * share], out_sems.at[buffer]
                    ).start()

        return reached

    reached = lax.fori_loop(0, count // GROUP, group, jnp.int32(1))
    ready(reached, NAB)
    for buffer in range(2):
        pltpu.make_async_copy(stage.at[buffer], outs[0].at[pl.ds(0, GROUP)], out_sems.at[buffer]).wait()


def expand_kernel(
    count, blocks, picks, got_ref, left_out, right_out, away_ref, own_ref,
    got, rows, keys, starts, weight, total, left, right, first, row_of, column_of, slot_of, stage,
    got_sems, copy_sems, out_sems,
):
    pairs = blocks * T
    sources = got_ref.shape[0]
    chunks = sources * count // T
    per = T // count
    batch = got.shape[1]
    rounds = sources // batch

    def arrival(r, buffer):
        return pltpu.make_async_copy(
            got_ref.at[pl.ds(r * batch, batch)], got.at[buffer], got_sems.at[buffer]
        )

    for r in range(2):
        arrival(r, r).start()
    sort_picks(picks, picks.shape[0] // 2, first, row_of, column_of, slot_of)
    rows[chunks * T :, :] = jnp.zeros((FIRST * T, 2 * T), BF16)
    keys[pl.ds(chunks, 8), :] = jnp.full((8, T), -1, jnp.int32)

    lanes = lax.broadcasted_iota(jnp.int32, (1, T), 1)

    def fill(r, carry):
        buffer = lax.rem(r, 2)
        arrival(r, buffer).wait()
        here = got.at[buffer]
        for j in range(batch // per):
            s = r * (batch // per) + j
            x = here[j * per : (j + 1) * per, 0:count, :].reshape(T, T)
            hi = x.astype(BF16)
            at = pl.ds(pl.multiple_of(s * T, T), T)
            rows[at, 0:T] = hi
            rows[at, T:] = (x - hi.astype(F32)).astype(BF16)
            key = here[j * per, count : count + 1, :]
            for i in range(1, per):
                key = jnp.where(lanes >= i * count, here[j * per + i, count : count + 1, :], key)
            keys[pl.ds(s, 1), :] = key.astype(jnp.int32)
        spread = here[:, count + 1, :]
        for f in range(FREQS):
            for n in range(blocks):
                lane = f * blocks + n
                weight[f, pl.ds(pl.multiple_of(n * T + r * batch, batch), batch), :] = jnp.broadcast_to(
                    spread[:, lane : lane + 1], (batch, T)
                )

        @pl.when(r + 2 < rounds)
        def _():
            arrival(r + 2, buffer).start()

        return carry

    lax.fori_loop(0, rounds, fill, 0)
    held = keys[0:chunks, :]
    for i in range(NAB + 1):
        starts[i] = jnp.sum((held < i * pairs).astype(jnp.int32))

    half = 2 * T
    wide = FIRST * T
    place = lax.broadcasted_iota(jnp.int32, (half, wide), 0)

    def put(a, n, value):
        at = slice(n * half, (n + 1) * half)

        turned = value.T
        hi = turned.astype(BF16)
        lo = (turned - hi.astype(F32)).astype(BF16)
        row = jnp.minimum(a, NAB - 2)
        left[row, 0:T, at] = hi
        left[row, T:, at] = lo
        slot = jnp.maximum(a, 1) - 1
        for f in range(FREQS):
            scaled = value * weight[f, at, :]
            hi = scaled.astype(BF16)
            cols = slice(f * T, (f + 1) * T)
            right[slot, 0, at, cols] = hi
            right[slot, 1, at, cols] = (scaled - hi.astype(F32)).astype(BF16)

    def column(a, carry):
        begin = starts[a]
        end = starts[a + 1]
        base = (begin // 16) * 16
        chunk = base // T
        more = end - base - wide

        near = jnp.concatenate([keys[pl.ds(chunk + j, 1), :] for j in range(FIRST + 1)], axis=1)
        near = jnp.broadcast_to(near, (8, wide + T))
        near = pltpu.roll(near, wide + T - (base - chunk * T), 1)
        key = near[0:1, 0:wide] - a * pairs
        source = rows[pl.ds(pl.multiple_of(base, 16), wide), :]
        for n in range(pairs // half):
            hot = jnp.where(place == key - n * half, 1.0, 0.0).astype(BF16)
            both = jnp.dot(hot, source, preferred_element_type=F32)
            put(a, n, both[:, 0:T] + both[:, T:])

        @pl.when(more > 0)
        def _():
            total[...] = jnp.zeros_like(total)

            def add(s, carry):
                key = keys[pl.ds(s, 1), :] - a * pairs
                for n in range(pairs // half):
                    hot = jnp.where(place[:, 0:T] == key - n * half, 1.0, 0.0).astype(BF16)
                    both = jnp.dot(
                        hot, rows[pl.ds(pl.multiple_of(s * T, T), T), :], preferred_element_type=F32
                    )
                    total[n * half : (n + 1) * half, :] += both[:, 0:T] + both[:, T:]
                return carry

            lax.fori_loop(chunk, (end + T - 1) // T, add, 0)
            for n in range(pairs // half):
                put(a, n, total[n * half : (n + 1) * half, :])

        @pl.when(a < NAB - 1)
        def _():
            pltpu.make_async_copy(left.at[a], left_out.at[a], copy_sems.at[0]).start()

        @pl.when(a >= 1)
        def _():
            pltpu.make_async_copy(right.at[a - 1], right_out.at[a - 1], copy_sems.at[1]).start()

        return carry

    lax.fori_loop(0, NAB - 2, column, 0)
    column(jnp.int32(NAB - 1), 0)
    column(jnp.int32(NAB - 2), 0)
    multiply(
        (row_of, column_of, slot_of), left, right, stage, (away_ref, own_ref), out_sems, lambda reached, need: need
    )
    pltpu.make_async_copy(left, left_out, copy_sems.at[0]).wait()
    pltpu.make_async_copy(right, right_out, copy_sems.at[1]).wait()


def expand(picks, got, count, blocks):
    sources = got.shape[0]
    chunks = sources * count // T
    pairs = blocks * T
    tiles = picks.shape[0]
    part = jax.ShapeDtypeStruct((tiles // 2, FREQS, T, T), F32)
    return pl.pallas_call(
        functools.partial(expand_kernel, count, blocks),
        grid_spec=pltpu.PrefetchScalarGridSpec(
            num_scalar_prefetch=1,
            grid=(),
            in_specs=[pl.BlockSpec(memory_space=pl.ANY)],
            out_specs=[pl.BlockSpec(memory_space=pl.ANY)] * 4,
            scratch_shapes=[
                pltpu.VMEM((2, 16) + got.shape[1:], F32),
                pltpu.VMEM(((chunks + FIRST) * T, 2 * T), BF16),
                pltpu.VMEM((chunks + 8, T), jnp.int32),
                pltpu.SMEM((NAB + 1,), jnp.int32),
                pltpu.VMEM((FREQS, pairs, T), F32),
                pltpu.VMEM((pairs, T), F32),
                pltpu.VMEM((NAB - 1, 2 * T, pairs), BF16),
                pltpu.VMEM((NAB - 1, 2, pairs, FREQS * T), BF16),
                pltpu.SMEM((NAB,), jnp.int32),
                pltpu.SMEM((tiles,), jnp.int32),
                pltpu.SMEM((tiles,), jnp.int32),
                pltpu.SMEM((tiles,), jnp.int32),
                pltpu.VMEM((2, GROUP, FREQS, T, T), F32),
                pltpu.SemaphoreType.DMA((2,)),
                pltpu.SemaphoreType.DMA((2,)),
                pltpu.SemaphoreType.DMA((2,)),
            ],
        ),
        out_shape=[
            jax.ShapeDtypeStruct((NAB - 1, 2 * T, pairs), BF16),
            jax.ShapeDtypeStruct((NAB - 1, 2, pairs, FREQS * T), BF16),
            part,
            part,
        ],
        compiler_params=pltpu.CompilerParams(vmem_limit_bytes=58 * MIB),
        name="expand",
    )(picks.reshape(-1), got)


def tiles_kernel(
    picks, left_ref, right_ref, away_ref, own_ref,
    left, right, first, row_of, column_of, slot_of, stage, left_sems, right_sems, out_sems,
):
    def fetch(q):
        return (
            pltpu.make_async_copy(left_ref.at[q - 1], left.at[q - 1], left_sems.at[q - 1]),
            pltpu.make_async_copy(right_ref.at[q - 1], right.at[q - 1], right_sems.at[q - 1]),
        )

    for q in range(1, AHEAD + 1):
        for copy in fetch(q):
            copy.start()
    sort_picks(picks, picks.shape[0] // 2, first, row_of, column_of, slot_of)

    def await_column(q, carry):
        @pl.when(q + AHEAD < NAB)
        def _():
            for copy in fetch(q + AHEAD):
                copy.start()

        for copy in fetch(q):
            copy.wait()
        return carry

    def ready(reached, need):
        lax.fori_loop(reached, need, await_column, 0)
        return need

    multiply((row_of, column_of, slot_of), left, right, stage, (away_ref, own_ref), out_sems, ready)


def tiles(picks, left, right):
    count = picks.shape[0]
    pairs = left.shape[2]
    part = jax.ShapeDtypeStruct((count // 2, FREQS, T, T), F32)
    return pl.pallas_call(
        tiles_kernel,
        grid_spec=pltpu.PrefetchScalarGridSpec(
            num_scalar_prefetch=1,
            grid=(),
            in_specs=[pl.BlockSpec(memory_space=pl.ANY)] * 2,
            out_specs=[pl.BlockSpec(memory_space=pl.ANY)] * 2,
            scratch_shapes=[
                pltpu.VMEM((NAB - 1, 2 * T, pairs), BF16),
                pltpu.VMEM((NAB - 1, 2, pairs, FREQS * T), BF16),
                pltpu.SMEM((NAB,), jnp.int32),
                pltpu.SMEM((count,), jnp.int32),
                pltpu.SMEM((count,), jnp.int32),
                pltpu.SMEM((count,), jnp.int32),
                pltpu.VMEM((2, GROUP, FREQS, T, T), F32),
                pltpu.SemaphoreType.DMA((NAB - 1,)),
                pltpu.SemaphoreType.DMA((NAB - 1,)),
                pltpu.SemaphoreType.DMA((2,)),
            ],
        ),
        out_shape=[part, part],
        compiler_params=pltpu.CompilerParams(vmem_limit_bytes=56 * MIB),
        cost_estimate=pl.CostEstimate(
            flops=6 * count * FREQS * T * T * pairs, bytes_accessed=56 * MIB, transcendentals=0
        ),
        name="tiles",
    )(picks.reshape(-1), left, right)


def layout(me, owner):
    plane = jnp.arange(16, dtype=jnp.int32)
    high, low = plane // 4, plane % 4
    here = jnp.where(owner == 0, me % 4, me // 32)
    lists = []
    for step in (2, 1, 3, 0):
        at = (here + step) % 4
        lists.append(
            jnp.where(owner == 0, ((high * 4 + low) * 2) * 4 + at, ((at * 4 + high) * 2 + 1) * 4 + low)
        )
    return lists


def shift(step):
    pairs = []
    for d in range(128):
        x, y, core, z = d // 32, d // 8 % 4, d // 4 % 2, d % 4
        if core == 0:
            z = (z + step) % 4
        else:
            x = (x + step) % 4
        pairs.append((d, ((x * 4 + y) * 2 + core) * 4 + z))
    return pairs


PLANES = [[(plane * 2) * 4 + z for plane in range(16)] for z in range(4)] + [
    [((x * 4 + plane // 4) * 2 + 1) * 4 + plane % 4 for plane in range(16)] for x in range(4)
]
SWAP = [(d, d ^ 4) for d in range(128)]


def on_device(b_tiles, tile_aux, tile_pair, freq_weights, kept):
    count = b_tiles.shape[0]
    devices = lax.axis_size("d")
    me = lax.axis_index("d")
    core = me // 4 % 2
    blocks = freq_weights.shape[1] // T

    sent = by_column(b_tiles, tile_aux, tile_pair, freq_weights, devices).reshape(devices, count + EXTRA, T)
    got = lax.all_to_all(sent, "d", split_axis=0, concat_axis=0, tiled=True)

    lists = [layout(me, owner) for owner in (1 - core, core)]
    picks = kept[
        jnp.concatenate(
            [part for far, up, down, keep in lists for part in (far, up[:8], down[:8])]
            + [part for far, up, down, keep in lists for part in (up[8:], down[8:], keep)]
        )
    ]
    left, right, away, own = expand(picks[:64], got, count, blocks)
    landed = lax.ppermute(away, "d", SWAP)
    leaving = [own[n] + landed[n] for n in (slice(0, 16), slice(16, 24), slice(24, 32))]
    left, right, leaving = lax.optimization_barrier((left, right, leaving))
    far = lax.ppermute(leaving[0], "d", shift(2))
    up_a = lax.ppermute(leaving[1], "d", shift(1))
    down_a = lax.ppermute(leaving[2], "d", shift(-1))

    away, own = tiles(picks[64:], left, right)
    away, far, up_a, down_a = lax.optimization_barrier((away, far, up_a, down_a))
    landed = lax.ppermute(away, "d", SWAP)
    up_b = lax.ppermute(own[0:8] + landed[0:8], "d", shift(1))
    down_b = lax.ppermute(own[8:16] + landed[8:16], "d", shift(-1))
    summed = jnp.concatenate(
        [
            own[16:24] + landed[16:24] + far[0:8] + up_a + down_a,
            own[24:32] + landed[24:32] + far[8:16] + up_b + down_b,
        ]
    )
    parts = lax.all_to_all(summed, "d", split_axis=0, concat_axis=0, tiled=True, axis_index_groups=PLANES)
    return jnp.sum(parts, axis=0, keepdims=True)


def solution(mesh):
    flat = Mesh(mesh.devices.reshape(-1), ("d",))
    placed = (P("d", None, None), P("d"), P("d"), P(None, "d"), P())
    return jax.shard_map(
        on_device, mesh=flat, in_specs=placed, out_specs=P("d", None, None, None), check_vma=False
    )
```

```python
import functools

import jax
import jax.numpy as jnp
from jax import lax
from jax.experimental import pallas as pl
from jax.experimental.pallas import tpu as pltpu
from jax.sharding import Mesh
from jax.sharding import PartitionSpec as P

NAB = 20
T = 128
FREQS = 2
EXTRA = 8
FIRST = 4
MIB = 1024 * 1024
ARRIVING = 4
BATCH = 16
GROUP = 16
BF16 = jnp.bfloat16
F32 = jnp.float32


def columns_kernel(groups, blocks, devices, tiles_ref, aux_ref, pair_ref, weights_ref, out_ref):
    step = pl.program_id(0)
    flat = out_ref.reshape(T * 8, T)

    @pl.when(step < groups)
    def _():
        for k in range(8):
            flat[pl.ds(k, T, stride=8), :] = tiles_ref[k].T

    @pl.when(step == groups)
    def _():
        out_ref[...] = jnp.zeros_like(out_ref)
        pair = pair_ref[...].astype(F32)
        source = jnp.floor((pair + 0.5) * (1.0 / blocks))
        key = aux_ref[...].astype(F32) * (blocks * devices) + (pair - source * blocks) * devices + source
        key = jnp.concatenate([key] * (T // key.shape[1]), axis=1)
        flat[pl.ds(0, T, stride=8), :] = jnp.broadcast_to(key, (T, T))
        rows = [weights_ref[f : f + 1, n * T : (n + 1) * T] for f in range(FREQS) for n in range(blocks)]
        rows.append(jnp.zeros((T - FREQS * blocks, T), F32))
        flat[pl.ds(1, T, stride=8), :] = jnp.concatenate(rows, axis=0).T


def by_column(b_tiles, aux, pair, weights, devices):
    count = b_tiles.shape[0]
    groups = count // 8
    blocks = weights.shape[1] // T
    return pl.pallas_call(
        functools.partial(columns_kernel, groups, blocks, devices),
        grid=(groups + 1,),
        in_specs=[
            pl.BlockSpec((8, T, T), lambda g: (jnp.minimum(g, groups - 1), 0, 0)),
            pl.BlockSpec((1, count), lambda g: (0, 0)),
            pl.BlockSpec((1, count), lambda g: (0, 0)),
            pl.BlockSpec(weights.shape, lambda g: (0, 0)),
        ],
        out_specs=pl.BlockSpec((T, None, 8, T), lambda g: (0, g, 0, 0)),
        out_shape=jax.ShapeDtypeStruct((T, groups + 1, 8, T), F32),
        name="columns",
    )(b_tiles, aux[None], pair[None], weights)


def multiply(picks, left, right, stage, outs, out_sems):
    share = outs[0].shape[0]

    def copies(g):
        buffer = lax.rem(g, 2)
        at = pl.ds(lax.rem(g, share // GROUP) * GROUP, GROUP)
        return [pltpu.make_async_copy(stage.at[buffer], out.at[at], out_sems.at[buffer]) for out in outs]

    def group(g, carry):
        buffer = lax.rem(g, 2)

        @pl.when(g >= 2)
        def _():
            copies(g)[0].wait()

        for k in range(GROUP):
            p = picks[2 * (g * GROUP + k)]
            q = picks[2 * (g * GROUP + k) + 1]
            both = jnp.dot(left[p], right[q, 0], preferred_element_type=F32)
            small = jnp.dot(left[p, 0:T, :], right[q, 1], preferred_element_type=F32)
            result = both[0:T] + (both[T:] + small)
            for f in range(FREQS):
                stage[buffer, k, f] = result[:, f * T : (f + 1) * T]
        for i, copy in enumerate(copies(g)):

            @pl.when(g // (share // GROUP) == i)
            def _():
                copy.start()

        return carry

    lax.fori_loop(0, len(outs) * share // GROUP, group, 0)
    for g in range(2):
        copies(g)[0].wait()


def products_kernel(count, blocks, shares, picks, got_ref, *refs):
    outs, (
        got, rows, keys, starts, weight, total, left, right, stage,
        got_sems, out_sems,
    ) = refs[:shares], refs[shares:]
    pairs = blocks * T
    sources = got_ref.shape[0]
    chunks = sources * count // T
    per = T // count
    batch = got.shape[1]
    rounds = sources // batch

    def arrival(r, buffer):
        return pltpu.make_async_copy(
            got_ref.at[pl.ds(r * batch, batch)], got.at[buffer], got_sems.at[buffer]
        )

    for r in range(ARRIVING):
        arrival(r, r).start()
    rows[chunks * T :, :] = jnp.zeros((FIRST * T, 2 * T), BF16)
    keys[pl.ds(chunks, 8), :] = jnp.full((8, T), -1, jnp.int32)

    lanes = lax.broadcasted_iota(jnp.int32, (1, T), 1)

    def fill(r, carry):
        buffer = lax.rem(r, ARRIVING)
        arrival(r, buffer).wait()
        here = got.at[buffer]
        for j in range(batch // per):
            s = r * (batch // per) + j
            x = here[j * per : (j + 1) * per, 0:count, :].reshape(T, T)
            hi = x.astype(BF16)
            at = pl.ds(pl.multiple_of(s * T, T), T)
            rows[at, 0:T] = hi
            rows[at, T:] = (x - hi.astype(F32)).astype(BF16)
            key = here[j * per, count : count + 1, :]
            for i in range(1, per):
                key = jnp.where(lanes >= i * count, here[j * per + i, count : count + 1, :], key)
            keys[pl.ds(s, 1), :] = key.astype(jnp.int32)
        spread = here[:, count + 1, :]
        for f in range(FREQS):
            for n in range(blocks):
                lane = f * blocks + n
                weight[f, pl.ds(pl.multiple_of(n * T + r * batch, batch), batch), :] = jnp.broadcast_to(
                    spread[:, lane : lane + 1], (batch, T)
                )

        @pl.when(r + ARRIVING < rounds)
        def _():
            arrival(r + ARRIVING, buffer).start()

        return carry

    lax.fori_loop(0, rounds, fill, 0)
    held = keys[0:chunks, :]
    for i in range(NAB + 1):
        starts[i] = jnp.sum((held < i * pairs).astype(jnp.int32))

    half = 2 * T
    wide = FIRST * T
    place = lax.broadcasted_iota(jnp.int32, (half, wide), 0)

    def put(a, n, value):
        at = slice(n * half, (n + 1) * half)

        turned = value.T
        hi = turned.astype(BF16)
        lo = (turned - hi.astype(F32)).astype(BF16)
        left[a, 0:T, at] = hi
        left[a, T:, at] = lo
        for f in range(FREQS):
            scaled = value * weight[f, at, :]
            hi = scaled.astype(BF16)
            cols = slice(f * T, (f + 1) * T)
            right[a, 0, at, cols] = hi
            right[a, 1, at, cols] = (scaled - hi.astype(F32)).astype(BF16)

    def straight(a):
        begin = starts[a]
        base = (begin // 16) * 16
        chunk = base // T
        near = jnp.concatenate([keys[pl.ds(chunk + j, 1), :] for j in range(FIRST + 1)], axis=1)
        near = jnp.broadcast_to(near, (8, wide + T))
        near = pltpu.roll(near, wide + T - (base - chunk * T), 1)
        key = near[0:1, 0:wide] - a * pairs
        source = rows[pl.ds(pl.multiple_of(base, 16), wide), :]
        for n in range(pairs // half):
            hot = jnp.where(place == key - n * half, 1.0, 0.0).astype(BF16)
            both = jnp.dot(hot, source, preferred_element_type=F32)
            put(a, n, both[:, 0:T] + both[:, T:])

    def whole(a):
        chunk = starts[a] // T
        end = starts[a + 1]

        @pl.when(end - (starts[a] // 16) * 16 > wide)
        def _():
            total[...] = jnp.zeros_like(total)

            def add(s, carry):
                key = keys[pl.ds(s, 1), :] - a * pairs
                for n in range(pairs // half):
                    hot = jnp.where(place[:, 0:T] == key - n * half, 1.0, 0.0).astype(BF16)
                    both = jnp.dot(
                        hot, rows[pl.ds(pl.multiple_of(s * T, T), T), :], preferred_element_type=F32
                    )
                    total[n * half : (n + 1) * half, :] += both[:, 0:T] + both[:, T:]
                return carry

            lax.fori_loop(chunk, (end + T - 1) // T, add, 0)
            for n in range(pairs // half):
                put(a, n, total[n * half : (n + 1) * half, :])

    def columns(i, carry):
        pair = 2 * i, 2 * i + 1
        for a in pair:
            straight(a)
        for a in pair:
            whole(a)
        return carry

    lax.fori_loop(0, NAB // 2, columns, 0)
    multiply(picks, left, right, stage, outs, out_sems)


def products(picks, shares, got, count, blocks):
    sources = got.shape[0]
    chunks = sources * count // T
    pairs = blocks * T
    tiles = picks.shape[0]
    return pl.pallas_call(
        functools.partial(products_kernel, count, blocks, shares),
        grid_spec=pltpu.PrefetchScalarGridSpec(
            num_scalar_prefetch=1,
            grid=(),
            in_specs=[pl.BlockSpec(memory_space=pl.ANY)],
            out_specs=[pl.BlockSpec(memory_space=pl.ANY)] * shares,
            scratch_shapes=[
                pltpu.VMEM((ARRIVING, BATCH) + got.shape[1:], F32),
                pltpu.VMEM(((chunks + FIRST) * T, 2 * T), BF16),
                pltpu.VMEM((chunks + 8, T), jnp.int32),
                pltpu.SMEM((NAB + 1,), jnp.int32),
                pltpu.VMEM((FREQS, pairs, T), F32),
                pltpu.VMEM((pairs, T), F32),
                pltpu.VMEM((NAB, 2 * T, pairs), BF16),
                pltpu.VMEM((NAB, 2, pairs, FREQS * T), BF16),
                pltpu.VMEM((2, GROUP, FREQS, T, T), F32),
                pltpu.SemaphoreType.DMA((ARRIVING,)),
                pltpu.SemaphoreType.DMA((2,)),
            ],
        ),
        out_shape=[jax.ShapeDtypeStruct((tiles // shares, FREQS, T, T), F32)] * shares,
        compiler_params=pltpu.CompilerParams(vmem_limit_bytes=61 * MIB),
        name="products",
    )(picks.reshape(-1), got)


def layout(me, owner):
    plane = jnp.arange(16, dtype=jnp.int32)
    high, low = plane // 4, plane % 4
    here = jnp.where(owner == 0, me % 4, me // 32)
    lists = []
    for step in (2, 1, 3, 0):
        at = (here + step) % 4
        lists.append(
            jnp.where(owner == 0, ((high * 4 + low) * 2) * 4 + at, ((at * 4 + high) * 2 + 1) * 4 + low)
        )
    return lists


def shift(step):
    pairs = []
    for d in range(128):
        x, y, core, z = d // 32, d // 8 % 4, d // 4 % 2, d % 4
        if core == 0:
            z = (z + step) % 4
        else:
            x = (x + step) % 4
        pairs.append((d, ((x * 4 + y) * 2 + core) * 4 + z))
    return pairs


PLANES = [[(plane * 2) * 4 + z for plane in range(16)] for z in range(4)] + [
    [((x * 4 + plane // 4) * 2 + 1) * 4 + plane % 4 for plane in range(16)] for x in range(4)
]
SWAP = [(d, d ^ 4) for d in range(128)]


def on_device(b_tiles, tile_aux, tile_pair, freq_weights, kept):
    count = b_tiles.shape[0]
    devices = lax.axis_size("d")
    me = lax.axis_index("d")
    core = me // 4 % 2
    blocks = freq_weights.shape[1] // T

    sent = by_column(b_tiles, tile_aux, tile_pair, freq_weights, devices).reshape(devices, count + EXTRA, T)
    got = lax.all_to_all(sent, "d", split_axis=0, concat_axis=0, tiled=True)

    far, up, down, keep = zip(*[layout(me, owner) for owner in (1 - core, core)])
    picks = kept[jnp.concatenate(far + up + down + keep)]
    partial = products(picks, 8, got, count, blocks)
    far, up, down, keep = [(own, lax.ppermute(away, "d", SWAP)) for away, own in zip(partial[0::2], partial[1::2])]
    low, high = slice(0, 8), slice(8, 16)

    def both(pair, part):
        return pair[0][part] + pair[1][part]

    from_below = lax.ppermute(both(far, low), "d", shift(1))
    from_above = lax.ppermute(both(far, high), "d", shift(-1))
    up_high = lax.ppermute(both(up, high), "d", shift(1))
    down_low = lax.ppermute(both(down, low), "d", shift(-1))
    up_low = lax.ppermute(both(up, low) + from_below, "d", shift(1))
    down_high = lax.ppermute(both(down, high) + from_above, "d", shift(-1))
    summed = jnp.concatenate([both(keep, low) + up_low + down_low, both(keep, high) + up_high + down_high])
    parts = lax.all_to_all(summed, "d", split_axis=0, concat_axis=0, tiled=True, axis_index_groups=PLANES)
    return jnp.sum(parts, axis=0, keepdims=True)


def solution(mesh):
    flat = Mesh(mesh.devices.reshape(-1), ("d",))
    placed = (P("d", None, None), P("d"), P("d"), P(None, "d"), P())
    return jax.shard_map(
        on_device, mesh=flat, in_specs=placed, out_specs=P("d", None, None, None), check_vma=False
    )
```

```python
import functools

import jax
import jax.numpy as jnp
from jax import lax
from jax.experimental import pallas as pl
from jax.experimental.pallas import tpu as pltpu
from jax.sharding import Mesh
from jax.sharding import PartitionSpec as P

NAB = 20
T = 128
FREQS = 2
EXTRA = 8
FIRST = 4
MIB = 1024 * 1024
ARRIVING = 4
BATCH = 16
KERNEL_MIB = 12
GROUP = 8
BF16 = jnp.bfloat16
F32 = jnp.float32


def columns_kernel(groups, blocks, devices, tiles_ref, aux_ref, pair_ref, weights_ref, out_ref):
    step = pl.program_id(0)
    flat = out_ref.reshape(T * 8, T)

    @pl.when(step < groups)
    def _():
        for k in range(8):
            flat[pl.ds(k, T, stride=8), :] = tiles_ref[k].T

    @pl.when(step == groups)
    def _():
        out_ref[...] = jnp.zeros_like(out_ref)
        pair = pair_ref[...].astype(F32)
        source = jnp.floor((pair + 0.5) * (1.0 / blocks))
        key = aux_ref[...].astype(F32) * (blocks * devices) + (pair - source * blocks) * devices + source
        key = jnp.concatenate([key] * (T // key.shape[1]), axis=1)
        flat[pl.ds(0, T, stride=8), :] = jnp.broadcast_to(key, (T, T))
        rows = [weights_ref[f : f + 1, n * T : (n + 1) * T] for f in range(FREQS) for n in range(blocks)]
        rows.append(jnp.zeros((T - FREQS * blocks, T), F32))
        flat[pl.ds(1, T, stride=8), :] = jnp.concatenate(rows, axis=0).T


def by_column(b_tiles, aux, pair, weights, devices):
    count = b_tiles.shape[0]
    groups = count // 8
    blocks = weights.shape[1] // T
    return pl.pallas_call(
        functools.partial(columns_kernel, groups, blocks, devices),
        grid=(groups + 1,),
        in_specs=[
            pl.BlockSpec((8, T, T), lambda g: (jnp.minimum(g, groups - 1), 0, 0)),
            pl.BlockSpec((1, count), lambda g: (0, 0)),
            pl.BlockSpec((1, count), lambda g: (0, 0)),
            pl.BlockSpec(weights.shape, lambda g: (0, 0)),
        ],
        out_specs=pl.BlockSpec((T, None, 8, T), lambda g: (0, g, 0, 0)),
        out_shape=jax.ShapeDtypeStruct((T, groups + 1, 8, T), F32),
        name="columns",
    )(b_tiles, aux[None], pair[None], weights)


def multiply(begin, picks, left, right, stage, outs, out_sems):
    share = outs[0].shape[0]

    def copies(g):
        buffer = lax.rem(g, 2)
        at = pl.ds(lax.rem(g, share // GROUP) * GROUP, GROUP)
        return [pltpu.make_async_copy(stage.at[buffer], out.at[at], out_sems.at[buffer]) for out in outs]

    def group(g, carry):
        buffer = lax.rem(g, 2)

        @pl.when(g >= 2)
        def _():
            copies(g)[0].wait()

        for k in range(GROUP):
            p = picks[2 * (begin + g * GROUP + k)]
            q = picks[2 * (begin + g * GROUP + k) + 1] - 1
            both = jnp.dot(left[p], right[q, 0], preferred_element_type=F32)
            small = jnp.dot(left[p, 0:T, :], right[q, 1], preferred_element_type=F32)
            result = both[0:T] + (both[T:] + small)
            for f in range(FREQS):
                stage[buffer, k, f] = result[:, f * T : (f + 1) * T]
        for i, copy in enumerate(copies(g)):

            @pl.when(g // (share // GROUP) == i)
            def _():
                copy.start()

        return carry

    lax.fori_loop(0, len(outs) * share // GROUP, group, 0)
    for g in range(2):
        copies(g)[0].wait()


def first_kernel(count, blocks, shares, picks, got_ref, left, right, *refs):
    outs, (
        got, rows, keys, starts, weight, total, stage,
        got_sems, out_sems,
    ) = refs[:shares], refs[shares:]
    pairs = blocks * T
    sources = got_ref.shape[0]
    chunks = sources * count // T
    per = T // count
    batch = got.shape[1]
    rounds = sources // batch

    def arrival(r, buffer):
        return pltpu.make_async_copy(
            got_ref.at[pl.ds(r * batch, batch)], got.at[buffer], got_sems.at[buffer]
        )

    for r in range(ARRIVING):
        arrival(r, r).start()
    rows[chunks * T :, :] = jnp.zeros((FIRST * T, 2 * T), BF16)
    keys[pl.ds(chunks, 8), :] = jnp.full((8, T), -1, jnp.int32)

    lanes = lax.broadcasted_iota(jnp.int32, (1, T), 1)

    def fill(r, carry):
        buffer = lax.rem(r, ARRIVING)
        arrival(r, buffer).wait()
        here = got.at[buffer]
        for j in range(batch // per):
            s = r * (batch // per) + j
            x = here[j * per : (j + 1) * per, 0:count, :].reshape(T, T)
            hi = x.astype(BF16)
            at = pl.ds(pl.multiple_of(s * T, T), T)
            rows[at, 0:T] = hi
            rows[at, T:] = (x - hi.astype(F32)).astype(BF16)
            key = here[j * per, count : count + 1, :]
            for i in range(1, per):
                key = jnp.where(lanes >= i * count, here[j * per + i, count : count + 1, :], key)
            keys[pl.ds(s, 1), :] = key.astype(jnp.int32)
        spread = here[:, count + 1, :]
        for f in range(FREQS):
            for n in range(blocks):
                lane = f * blocks + n
                weight[f, pl.ds(pl.multiple_of(n * T + r * batch, batch), batch), :] = jnp.broadcast_to(
                    spread[:, lane : lane + 1], (batch, T)
                )

        @pl.when(r + ARRIVING < rounds)
        def _():
            arrival(r + ARRIVING, buffer).start()

        return carry

    lax.fori_loop(0, rounds, fill, 0)
    held = keys[0:chunks, :]
    for i in range(NAB + 1):
        starts[i] = jnp.sum((held < i * pairs).astype(jnp.int32))

    half = 2 * T
    wide = FIRST * T
    place = lax.broadcasted_iota(jnp.int32, (half, wide), 0)

    def put(a, n, value):
        at = slice(n * half, (n + 1) * half)

        row = jnp.minimum(a, NAB - 2)
        slot = jnp.maximum(a, 1) - 1
        turned = value.T
        hi = turned.astype(BF16)
        lo = (turned - hi.astype(F32)).astype(BF16)
        left[row, 0:T, at] = hi
        left[row, T:, at] = lo
        for f in range(FREQS):
            scaled = value * weight[f, at, :]
            hi = scaled.astype(BF16)
            cols = slice(f * T, (f + 1) * T)
            right[slot, 0, at, cols] = hi
            right[slot, 1, at, cols] = (scaled - hi.astype(F32)).astype(BF16)

    def straight(a):
        begin = starts[a]
        base = (begin // 16) * 16
        chunk = base // T
        near = jnp.concatenate([keys[pl.ds(chunk + j, 1), :] for j in range(FIRST + 1)], axis=1)
        near = jnp.broadcast_to(near, (8, wide + T))
        near = pltpu.roll(near, wide + T - (base - chunk * T), 1)
        key = near[0:1, 0:wide] - a * pairs
        source = rows[pl.ds(pl.multiple_of(base, 16), wide), :]
        for n in range(pairs // half):
            hot = jnp.where(place == key - n * half, 1.0, 0.0).astype(BF16)
            both = jnp.dot(hot, source, preferred_element_type=F32)
            put(a, n, both[:, 0:T] + both[:, T:])

    def whole(a):
        total[...] = jnp.zeros_like(total)

        def add(s, carry):
            key = keys[pl.ds(s, 1), :] - a * pairs
            for n in range(pairs // half):
                hot = jnp.where(place[:, 0:T] == key - n * half, 1.0, 0.0).astype(BF16)
                both = jnp.dot(hot, rows[pl.ds(pl.multiple_of(s * T, T), T), :], preferred_element_type=F32)
                total[n * half : (n + 1) * half, :] += both[:, 0:T] + both[:, T:]
            return carry

        lax.fori_loop(starts[a] // T, (starts[a + 1] + T - 1) // T, add, 0)
        for n in range(pairs // half):
            put(a, n, total[n * half : (n + 1) * half, :])

    def beyond(a):
        return starts[a + 1] - (starts[a] // 16) * 16 > wide

    def columns(i, carry):
        last = 2 * i == NAB - 2
        pair = jnp.where(last, NAB - 1, 2 * i), jnp.where(last, NAB - 2, 2 * i + 1)
        for a in pair:
            straight(a)

        @pl.when(jnp.logical_or(beyond(pair[0]), beyond(pair[1])))
        def _():
            for a in pair:
                whole(a)

        return carry

    lax.fori_loop(0, NAB // 2, columns, 0)
    multiply(0, picks, left, right, stage, outs, out_sems)


def first_products(picks, tiles, got, count, blocks):
    sources = got.shape[0]
    chunks = sources * count // T
    pairs = blocks * T
    shares = 2
    return pl.pallas_call(
        functools.partial(first_kernel, count, blocks, shares),
        grid_spec=pltpu.PrefetchScalarGridSpec(
            num_scalar_prefetch=1,
            grid=(),
            in_specs=[pl.BlockSpec(memory_space=pl.ANY)],
            out_specs=[pl.BlockSpec(memory_space=pltpu.VMEM)] * 2 + [pl.BlockSpec(memory_space=pl.ANY)] * shares,
            scratch_shapes=[
                pltpu.VMEM((ARRIVING, BATCH) + got.shape[1:], F32),
                pltpu.VMEM(((chunks + FIRST) * T, 2 * T), BF16),
                pltpu.VMEM((chunks + 8, T), jnp.int32),
                pltpu.SMEM((NAB + 1,), jnp.int32),
                pltpu.VMEM((FREQS, pairs, T), F32),
                pltpu.VMEM((pairs, T), F32),
                pltpu.VMEM((2, GROUP, FREQS, T, T), F32),
                pltpu.SemaphoreType.DMA((ARRIVING,)),
                pltpu.SemaphoreType.DMA((2,)),
            ],
        ),
        out_shape=[
            pltpu.VMEM((NAB - 1, 2 * T, pairs), BF16),
            pltpu.VMEM((NAB - 1, 2, pairs, FREQS * T), BF16),
        ]
        + [jax.ShapeDtypeStruct((tiles // shares, FREQS, T, T), F32)] * shares,
        compiler_params=pltpu.CompilerParams(vmem_limit_bytes=KERNEL_MIB * MIB),
        name="first_products",
    )(picks, got)


def more_kernel(at, fences, picks, left, right, *refs):
    outs, (stage, out_sems) = refs[fences:-2], refs[-2:]
    multiply(at, picks, left, right, stage, outs, out_sems)


def more_products(at, picks, left, right, fence=()):
    return pl.pallas_call(
        functools.partial(more_kernel, at, len(fence)),
        grid_spec=pltpu.PrefetchScalarGridSpec(
            num_scalar_prefetch=1,
            grid=(),
            in_specs=[pl.BlockSpec(memory_space=pltpu.VMEM)] * 2
            + [pl.BlockSpec(memory_space=pl.ANY)] * len(fence),
            out_specs=[pl.BlockSpec(memory_space=pl.ANY)] * 2,
            scratch_shapes=[
                pltpu.VMEM((2, GROUP, FREQS, T, T), F32),
                pltpu.SemaphoreType.DMA((2,)),
            ],
        ),
        out_shape=[jax.ShapeDtypeStruct((16, FREQS, T, T), F32)] * 2,
        compiler_params=pltpu.CompilerParams(vmem_limit_bytes=KERNEL_MIB * MIB),
        cost_estimate=pl.CostEstimate(
            flops=12 * GROUP * FREQS * T * T * left.shape[2], bytes_accessed=4 * MIB, transcendentals=0
        ),
        name="more_products",
    )(
        picks,
        pltpu.with_memory_space_constraint(left, pltpu.VMEM),
        pltpu.with_memory_space_constraint(right, pltpu.VMEM),
        *fence,
    )


def add_kernel(a_low, a_high, b_low, b_high, low, high):
    low[...] = a_low[...] + b_low[...]
    high[...] = a_high[...] + b_high[...]


def add_halves(a, b):
    half = a.shape[0] // 2
    step = 2
    block = (step,) + a.shape[1:]
    first = pl.BlockSpec(block, lambda i: (i, 0, 0, 0))
    second = pl.BlockSpec(block, lambda i: (i + half // step, 0, 0, 0))
    return pl.pallas_call(
        add_kernel,
        grid=(half // step,),
        in_specs=[first, second, first, second],
        out_specs=[first, first],
        out_shape=[jax.ShapeDtypeStruct((half,) + a.shape[1:], F32)] * 2,
        compiler_params=pltpu.CompilerParams(vmem_limit_bytes=KERNEL_MIB * MIB),
        name="add_halves",
    )(a, a, b, b)


def layout(me, owner):
    plane = jnp.arange(16, dtype=jnp.int32)
    high, low = plane // 4, plane % 4
    here = jnp.where(owner == 0, me % 4, me // 32)
    lists = []
    for step in (2, 1, 3, 0):
        at = (here + step) % 4
        lists.append(
            jnp.where(owner == 0, ((high * 4 + low) * 2) * 4 + at, ((at * 4 + high) * 2 + 1) * 4 + low)
        )
    return lists


def shift(step):
    pairs = []
    for d in range(128):
        x, y, core, z = d // 32, d // 8 % 4, d // 4 % 2, d % 4
        if core == 0:
            z = (z + step) % 4
        else:
            x = (x + step) % 4
        pairs.append((d, ((x * 4 + y) * 2 + core) * 4 + z))
    return pairs


PLANES = [[(plane * 2) * 4 + z for plane in range(16)] for z in range(4)] + [
    [((x * 4 + plane // 4) * 2 + 1) * 4 + plane % 4 for plane in range(16)] for x in range(4)
]
SWAP = [(d, d ^ 4) for d in range(128)]


def on_device(b_tiles, tile_aux, tile_pair, freq_weights, kept):
    count = b_tiles.shape[0]
    devices = lax.axis_size("d")
    me = lax.axis_index("d")
    core = me // 4 % 2
    blocks = freq_weights.shape[1] // T

    sent = by_column(b_tiles, tile_aux, tile_pair, freq_weights, devices).reshape(devices, count + EXTRA, T)
    got = lax.all_to_all(sent, "d", split_axis=0, concat_axis=0, tiled=True)

    far, up, down, keep = zip(*[layout(me, owner) for owner in (1 - core, core)])
    low, high = slice(0, 8), slice(8, 16)
    lists = [
        [far[0], far[1]],
        [up[0][high], down[0][low], up[1][high], down[1][low]],
        [up[0][low], down[0][high], up[1][low], down[1][high]],
        [keep[0], keep[1]],
    ]
    picks = kept[jnp.concatenate([part for some in lists for part in some])].reshape(-1)

    def swap(tiles):
        return lax.ppermute(tiles, "d", SWAP)

    def send(pair):
        return [lax.ppermute(part, "d", shift(step)) for part, step in zip(pair, (1, -1))]

    left, right, away, far = first_products(picks, 32, got, count, blocks)
    landed = swap(away)
    away, second = more_products(32, picks, left, right)
    away, landed = lax.optimization_barrier((away, landed))

    leaving = add_halves(far, landed)
    passing = send(leaving)
    landed = swap(away)
    away, third = more_products(64, picks, left, right, leaving)
    away, landed, passing = lax.optimization_barrier((away, landed, passing))

    leaving = add_halves(second, landed)
    arrived = send(leaving)
    landed = swap(away)
    away, keep = more_products(96, picks, left, right, leaving)
    away, landed, arrived = lax.optimization_barrier((away, landed, arrived))

    last = send([third[low] + landed[low] + passing[0], third[high] + landed[high] + passing[1]])
    landed = swap(away)
    summed = jnp.concatenate(
        [
            keep[low] + landed[low] + last[0] + arrived[1],
            keep[high] + landed[high] + last[1] + arrived[0],
        ]
    )
    parts = lax.all_to_all(summed, "d", split_axis=0, concat_axis=0, tiled=True, axis_index_groups=PLANES)
    return jnp.sum(parts, axis=0, keepdims=True)


def solution(mesh):
    flat = Mesh(mesh.devices.reshape(-1), ("d",))
    placed = (P("d", None, None), P("d"), P("d"), P(None, "d"), P())
    return jax.shard_map(
        on_device, mesh=flat, in_specs=placed, out_specs=P("d", None, None, None), check_vma=False
    )
```

```python
import functools

import jax
import jax.numpy as jnp
from jax import lax
from jax.experimental import pallas as pl
from jax.experimental.pallas import tpu as pltpu
from jax.sharding import Mesh
from jax.sharding import PartitionSpec as P

NAB = 20
T = 128
FREQS = 2
EXTRA = 8
FIRST = 4
MIB = 1024 * 1024
ARRIVING = 4
BATCH = 16
KERNEL_MIB = 12
GROUP = 8
BF16 = jnp.bfloat16
F32 = jnp.float32


def columns_kernel(groups, blocks, devices, tiles_ref, aux_ref, pair_ref, weights_ref, out_ref):
    step = pl.program_id(0)
    flat = out_ref.reshape(T * 8, T)

    @pl.when(step < groups)
    def _():
        for k in range(8):
            flat[pl.ds(k, T, stride=8), :] = tiles_ref[k].T

    @pl.when(step == groups)
    def _():
        out_ref[...] = jnp.zeros_like(out_ref)
        pair = pair_ref[...].astype(F32)
        source = jnp.floor((pair + 0.5) * (1.0 / blocks))
        key = aux_ref[...].astype(F32) * (blocks * devices) + (pair - source * blocks) * devices + source
        key = jnp.concatenate([key] * (T // key.shape[1]), axis=1)
        flat[pl.ds(0, T, stride=8), :] = jnp.broadcast_to(key, (T, T))
        rows = [weights_ref[f : f + 1, n * T : (n + 1) * T] for f in range(FREQS) for n in range(blocks)]
        rows.append(jnp.zeros((T - FREQS * blocks, T), F32))
        flat[pl.ds(1, T, stride=8), :] = jnp.concatenate(rows, axis=0).T


def by_column(b_tiles, aux, pair, weights, devices):
    count = b_tiles.shape[0]
    groups = count // 8
    blocks = weights.shape[1] // T
    return pl.pallas_call(
        functools.partial(columns_kernel, groups, blocks, devices),
        grid=(groups + 1,),
        in_specs=[
            pl.BlockSpec((8, T, T), lambda g: (jnp.minimum(g, groups - 1), 0, 0)),
            pl.BlockSpec((1, count), lambda g: (0, 0)),
            pl.BlockSpec((1, count), lambda g: (0, 0)),
            pl.BlockSpec(weights.shape, lambda g: (0, 0)),
        ],
        out_specs=pl.BlockSpec((T, None, 8, T), lambda g: (0, g, 0, 0)),
        out_shape=jax.ShapeDtypeStruct((T, groups + 1, 8, T), F32),
        name="columns",
    )(b_tiles, aux[None], pair[None], weights)


def multiply(begin, picks, left, right, stage, outs, out_sems):
    share = outs[0].shape[0]

    def copies(g):
        buffer = lax.rem(g, 2)
        at = pl.ds(lax.rem(g, share // GROUP) * GROUP, GROUP)
        return [pltpu.make_async_copy(stage.at[buffer], out.at[at], out_sems.at[buffer]) for out in outs]

    def group(g, carry):
        buffer = lax.rem(g, 2)

        @pl.when(g >= 2)
        def _():
            copies(g)[0].wait()

        for k in range(GROUP):
            p = picks[2 * (begin + g * GROUP + k)]
            q = picks[2 * (begin + g * GROUP + k) + 1] - 1
            both = jnp.dot(left[p], right[q, 0], preferred_element_type=F32)
            small = jnp.dot(left[p, 0:T, :], right[q, 1], preferred_element_type=F32)
            result = both[0:T] + (both[T:] + small)
            for f in range(FREQS):
                stage[buffer, k, f] = result[:, f * T : (f + 1) * T]
        for i, copy in enumerate(copies(g)):

            @pl.when(g // (share // GROUP) == i)
            def _():
                copy.start()

        return carry

    lax.fori_loop(0, len(outs) * share // GROUP, group, 0)
    for g in range(2):
        copies(g)[0].wait()


def first_kernel(count, blocks, shares, picks, got_ref, left, right, *refs):
    outs, (
        got, rows, keys, starts, weight, total, stage,
        got_sems, out_sems,
    ) = refs[:shares], refs[shares:]
    pairs = blocks * T
    sources = got_ref.shape[0]
    chunks = sources * count // T
    per = T // count
    batch = got.shape[1]
    rounds = sources // batch

    def arrival(r, buffer):
        return pltpu.make_async_copy(
            got_ref.at[pl.ds(r * batch, batch)], got.at[buffer], got_sems.at[buffer]
        )

    for r in range(ARRIVING):
        arrival(r, r).start()
    rows[chunks * T :, :] = jnp.zeros((FIRST * T, 2 * T), BF16)
    keys[pl.ds(chunks, 8), :] = jnp.full((8, T), -1, jnp.int32)

    lanes = lax.broadcasted_iota(jnp.int32, (1, T), 1)

    def fill(r, carry):
        buffer = lax.rem(r, ARRIVING)
        arrival(r, buffer).wait()
        here = got.at[buffer]
        for j in range(batch // per):
            s = r * (batch // per) + j
            x = here[j * per : (j + 1) * per, 0:count, :].reshape(T, T)
            hi = x.astype(BF16)
            at = pl.ds(pl.multiple_of(s * T, T), T)
            rows[at, 0:T] = hi
            rows[at, T:] = (x - hi.astype(F32)).astype(BF16)
            key = here[j * per, count : count + 1, :]
            for i in range(1, per):
                key = jnp.where(lanes >= i * count, here[j * per + i, count : count + 1, :], key)
            keys[pl.ds(s, 1), :] = key.astype(jnp.int32)
        spread = here[:, count + 1, :]
        for f in range(FREQS):
            for n in range(blocks):
                lane = f * blocks + n
                weight[f, pl.ds(pl.multiple_of(n * T + r * batch, batch), batch), :] = jnp.broadcast_to(
                    spread[:, lane : lane + 1], (batch, T)
                )

        @pl.when(r + ARRIVING < rounds)
        def _():
            arrival(r + ARRIVING, buffer).start()

        return carry

    lax.fori_loop(0, rounds, fill, 0)
    held = keys[0:chunks, :]
    for i in range(NAB + 1):
        starts[i] = jnp.sum((held < i * pairs).astype(jnp.int32))

    half = 2 * T
    wide = FIRST * T
    place = lax.broadcasted_iota(jnp.int32, (half, wide), 0)

    def put(a, n, value):
        at = slice(n * half, (n + 1) * half)

        row = jnp.minimum(a, NAB - 2)
        slot = jnp.maximum(a, 1) - 1
        turned = value.T
        hi = turned.astype(BF16)
        lo = (turned - hi.astype(F32)).astype(BF16)
        left[row, 0:T, at] = hi
        left[row, T:, at] = lo
        for f in range(FREQS):
            scaled = value * weight[f, at, :]
            hi = scaled.astype(BF16)
            cols = slice(f * T, (f + 1) * T)
            right[slot, 0, at, cols] = hi
            right[slot, 1, at, cols] = (scaled - hi.astype(F32)).astype(BF16)

    def straight(a):
        begin = starts[a]
        base = (begin // 16) * 16
        chunk = base // T
        near = jnp.concatenate([keys[pl.ds(chunk + j, 1), :] for j in range(FIRST + 1)], axis=1)
        near = jnp.broadcast_to(near, (8, wide + T))
        near = pltpu.roll(near, wide + T - (base - chunk * T), 1)
        key = near[0:1, 0:wide] - a * pairs
        source = rows[pl.ds(pl.multiple_of(base, 16), wide), :]
        for n in range(pairs // half):
            hot = jnp.where(place == key - n * half, 1.0, 0.0).astype(BF16)
            both = jnp.dot(hot, source, preferred_element_type=F32)
            put(a, n, both[:, 0:T] + both[:, T:])

    def whole(a):
        total[...] = jnp.zeros_like(total)

        def add(s, carry):
            key = keys[pl.ds(s, 1), :] - a * pairs
            for n in range(pairs // half):
                hot = jnp.where(place[:, 0:T] == key - n * half, 1.0, 0.0).astype(BF16)
                both = jnp.dot(hot, rows[pl.ds(pl.multiple_of(s * T, T), T), :], preferred_element_type=F32)
                total[n * half : (n + 1) * half, :] += both[:, 0:T] + both[:, T:]
            return carry

        lax.fori_loop(starts[a] // T, (starts[a + 1] + T - 1) // T, add, 0)
        for n in range(pairs // half):
            put(a, n, total[n * half : (n + 1) * half, :])

    def beyond(a):
        return starts[a + 1] - (starts[a] // 16) * 16 > wide

    def columns(i, carry):
        last = 2 * i == NAB - 2
        pair = jnp.where(last, NAB - 1, 2 * i), jnp.where(last, NAB - 2, 2 * i + 1)
        for a in pair:
            straight(a)

        @pl.when(jnp.logical_or(beyond(pair[0]), beyond(pair[1])))
        def _():
            for a in pair:
                whole(a)

        return carry

    lax.fori_loop(0, NAB // 2, columns, 0)
    multiply(0, picks, left, right, stage, outs, out_sems)


def first_products(picks, tiles, got, count, blocks):
    sources = got.shape[0]
    chunks = sources * count // T
    pairs = blocks * T
    shares = 2
    return pl.pallas_call(
        functools.partial(first_kernel, count, blocks, shares),
        grid_spec=pltpu.PrefetchScalarGridSpec(
            num_scalar_prefetch=1,
            grid=(),
            in_specs=[pl.BlockSpec(memory_space=pl.ANY)],
            out_specs=[pl.BlockSpec(memory_space=pltpu.VMEM)] * 2 + [pl.BlockSpec(memory_space=pl.ANY)] * shares,
            scratch_shapes=[
                pltpu.VMEM((ARRIVING, BATCH) + got.shape[1:], F32),
                pltpu.VMEM(((chunks + FIRST) * T, 2 * T), BF16),
                pltpu.VMEM((chunks + 8, T), jnp.int32),
                pltpu.SMEM((NAB + 1,), jnp.int32),
                pltpu.VMEM((FREQS, pairs, T), F32),
                pltpu.VMEM((pairs, T), F32),
                pltpu.VMEM((2, GROUP, FREQS, T, T), F32),
                pltpu.SemaphoreType.DMA((ARRIVING,)),
                pltpu.SemaphoreType.DMA((2,)),
            ],
        ),
        out_shape=[
            pltpu.VMEM((NAB - 1, 2 * T, pairs), BF16),
            pltpu.VMEM((NAB - 1, 2, pairs, FREQS * T), BF16),
        ]
        + [pltpu.HBM((tiles // shares, FREQS, T, T), F32)] * shares,
        compiler_params=pltpu.CompilerParams(vmem_limit_bytes=KERNEL_MIB * MIB),
        name="first_products",
    )(picks, got)


def more_kernel(at, fences, picks, left, right, *refs):
    outs, (stage, out_sems) = refs[fences:-2], refs[-2:]
    multiply(at, picks, left, right, stage, outs, out_sems)


def more_products(at, picks, left, right, fence=()):
    return pl.pallas_call(
        functools.partial(more_kernel, at, len(fence)),
        grid_spec=pltpu.PrefetchScalarGridSpec(
            num_scalar_prefetch=1,
            grid=(),
            in_specs=[pl.BlockSpec(memory_space=pltpu.VMEM)] * 2
            + [pl.BlockSpec(memory_space=pl.ANY)] * len(fence),
            out_specs=[pl.BlockSpec(memory_space=pl.ANY)] * 2,
            scratch_shapes=[
                pltpu.VMEM((2, GROUP, FREQS, T, T), F32),
                pltpu.SemaphoreType.DMA((2,)),
            ],
        ),
        out_shape=[pltpu.HBM((16, FREQS, T, T), F32)] * 2,
        compiler_params=pltpu.CompilerParams(vmem_limit_bytes=KERNEL_MIB * MIB),
        cost_estimate=pl.CostEstimate(
            flops=12 * GROUP * FREQS * T * T * left.shape[2], bytes_accessed=4 * MIB, transcendentals=0
        ),
        name="more_products",
    )(
        picks,
        pltpu.with_memory_space_constraint(left, pltpu.VMEM),
        pltpu.with_memory_space_constraint(right, pltpu.VMEM),
        *fence,
    )


def add_kernel(a_low, a_high, b_low, b_high, low, high):
    low[...] = a_low[...] + b_low[...]
    high[...] = a_high[...] + b_high[...]


def add_halves(a, b):
    half = a.shape[0] // 2
    step = 2
    a = pltpu.with_memory_space_constraint(a, pltpu.HBM)
    b = pltpu.with_memory_space_constraint(b, pltpu.HBM)
    block = (step,) + a.shape[1:]
    first = pl.BlockSpec(block, lambda i: (i, 0, 0, 0))
    second = pl.BlockSpec(block, lambda i: (i + half // step, 0, 0, 0))
    return pl.pallas_call(
        add_kernel,
        grid=(half // step,),
        in_specs=[first, second, first, second],
        out_specs=[first, first],
        out_shape=[pltpu.HBM((half,) + a.shape[1:], F32)] * 2,
        compiler_params=pltpu.CompilerParams(vmem_limit_bytes=KERNEL_MIB * MIB),
        name="add_halves",
    )(a, a, b, b)


def layout(me, owner):
    plane = jnp.arange(16, dtype=jnp.int32)
    high, low = plane // 4, plane % 4
    here = jnp.where(owner == 0, me % 4, me // 32)
    lists = []
    for step in (2, 1, 3, 0):
        at = (here + step) % 4
        lists.append(
            jnp.where(owner == 0, ((high * 4 + low) * 2) * 4 + at, ((at * 4 + high) * 2 + 1) * 4 + low)
        )
    return lists


def shift(step):
    pairs = []
    for d in range(128):
        x, y, core, z = d // 32, d // 8 % 4, d // 4 % 2, d % 4
        if core == 0:
            z = (z + step) % 4
        else:
            x = (x + step) % 4
        pairs.append((d, ((x * 4 + y) * 2 + core) * 4 + z))
    return pairs


PLANES = [[(plane * 2) * 4 + z for plane in range(16)] for z in range(4)] + [
    [((x * 4 + plane // 4) * 2 + 1) * 4 + plane % 4 for plane in range(16)] for x in range(4)
]
SWAP = [(d, d ^ 4) for d in range(128)]


def on_device(b_tiles, tile_aux, tile_pair, freq_weights, kept):
    count = b_tiles.shape[0]
    devices = lax.axis_size("d")
    me = lax.axis_index("d")
    core = me // 4 % 2
    blocks = freq_weights.shape[1] // T

    sent = by_column(b_tiles, tile_aux, tile_pair, freq_weights, devices).reshape(devices, count + EXTRA, T)
    got = lax.all_to_all(sent, "d", split_axis=0, concat_axis=0, tiled=True)

    far, up, down, keep = zip(*[layout(me, owner) for owner in (1 - core, core)])
    low, high = slice(0, 8), slice(8, 16)
    lists = [
        [far[0], far[1]],
        [up[0][high], down[0][low], up[1][high], down[1][low]],
        [up[0][low], down[0][high], up[1][low], down[1][high]],
        [keep[0], keep[1]],
    ]
    picks = kept[jnp.concatenate([part for some in lists for part in some])].reshape(-1)

    def swap(tiles):
        return lax.ppermute(tiles, "d", SWAP)

    def send(pair):
        return [lax.ppermute(part, "d", shift(step)) for part, step in zip(pair, (1, -1))]

    left, right, away, far = first_products(picks, 32, got, count, blocks)
    landed = swap(away)
    away, second = more_products(32, picks, left, right)
    away, landed = lax.optimization_barrier((away, landed))

    leaving = add_halves(far, landed)
    passing = send(leaving)
    landed = swap(away)
    away, third = more_products(64, picks, left, right, leaving)
    away, landed, passing = lax.optimization_barrier((away, landed, passing))

    leaving = add_halves(second, landed)
    arrived = send(leaving)
    landed = swap(away)
    away, keep = more_products(96, picks, left, right, leaving)
    away, landed, arrived = lax.optimization_barrier((away, landed, arrived))

    last = send([third[low] + landed[low] + passing[0], third[high] + landed[high] + passing[1]])
    landed = swap(away)
    summed = jnp.concatenate(
        [
            keep[low] + landed[low] + last[0] + arrived[1],
            keep[high] + landed[high] + last[1] + arrived[0],
        ]
    )
    parts = lax.all_to_all(summed, "d", split_axis=0, concat_axis=0, tiled=True, axis_index_groups=PLANES)
    return jnp.sum(parts, axis=0, keepdims=True)


def solution(mesh):
    flat = Mesh(mesh.devices.reshape(-1), ("d",))
    placed = (P("d", None, None), P("d"), P("d"), P(None, "d"), P())
    return jax.shard_map(
        on_device, mesh=flat, in_specs=placed, out_specs=P("d", None, None, None), check_vma=False
    )
```

```python
import functools

import jax
import jax.numpy as jnp
from jax import lax
from jax.experimental import pallas as pl
from jax.experimental.pallas import tpu as pltpu
from jax.sharding import Mesh
from jax.sharding import PartitionSpec as P

NAB = 20
T = 128
FREQS = 2
EXTRA = 8
FIRST = 4
MIB = 1024 * 1024
ARRIVING = 4
BATCH = 16
KERNEL_MIB = 12
GROUP = 8
BF16 = jnp.bfloat16
F32 = jnp.float32


def columns_kernel(groups, blocks, devices, tiles_ref, aux_ref, pair_ref, weights_ref, out_ref):
    step = pl.program_id(0)
    flat = out_ref.reshape(T * 8, T)

    @pl.when(step < groups)
    def _():
        for k in range(8):
            flat[pl.ds(k, T, stride=8), :] = tiles_ref[k].T

    @pl.when(step == groups)
    def _():
        out_ref[...] = jnp.zeros_like(out_ref)
        pair = pair_ref[...].astype(F32)
        source = jnp.floor((pair + 0.5) * (1.0 / blocks))
        key = aux_ref[...].astype(F32) * (blocks * devices) + (pair - source * blocks) * devices + source
        key = jnp.concatenate([key] * (T // key.shape[1]), axis=1)
        flat[pl.ds(0, T, stride=8), :] = jnp.broadcast_to(key, (T, T))
        rows = [weights_ref[f : f + 1, n * T : (n + 1) * T] for f in range(FREQS) for n in range(blocks)]
        rows.append(jnp.zeros((T - FREQS * blocks, T), F32))
        flat[pl.ds(1, T, stride=8), :] = jnp.concatenate(rows, axis=0).T


def by_column(b_tiles, aux, pair, weights, devices):
    count = b_tiles.shape[0]
    groups = count // 8
    blocks = weights.shape[1] // T
    return pl.pallas_call(
        functools.partial(columns_kernel, groups, blocks, devices),
        grid=(groups + 1,),
        in_specs=[
            pl.BlockSpec((8, T, T), lambda g: (jnp.minimum(g, groups - 1), 0, 0)),
            pl.BlockSpec((1, count), lambda g: (0, 0)),
            pl.BlockSpec((1, count), lambda g: (0, 0)),
            pl.BlockSpec(weights.shape, lambda g: (0, 0)),
        ],
        out_specs=pl.BlockSpec((T, None, 8, T), lambda g: (0, g, 0, 0)),
        out_shape=jax.ShapeDtypeStruct((T, groups + 1, 8, T), F32),
        name="columns",
    )(b_tiles, aux[None], pair[None], weights)


def multiply(begin, picks, left, right, stage, outs, out_sems):
    share = outs[0].shape[0]
    size = stage.shape[1]

    def copies(g):
        buffer = lax.rem(g, 2)
        at = pl.ds(lax.rem(g, share // size) * size, size)
        return [pltpu.make_async_copy(stage.at[buffer], out.at[at], out_sems.at[buffer]) for out in outs]

    def group(g, carry):
        buffer = lax.rem(g, 2)

        @pl.when(g >= 2)
        def _():
            copies(g)[0].wait()

        for k in range(size):
            p = picks[2 * (begin + g * size + k)]
            q = picks[2 * (begin + g * size + k) + 1] - 1
            both = jnp.dot(left[p], right[q, 0], preferred_element_type=F32)
            small = jnp.dot(left[p, 0:T, :], right[q, 1], preferred_element_type=F32)
            result = both[0:T] + (both[T:] + small)
            for f in range(FREQS):
                stage[buffer, k, f] = result[:, f * T : (f + 1) * T]
        for i, copy in enumerate(copies(g)):

            @pl.when(g // (share // size) == i)
            def _():
                copy.start()

        return carry

    lax.fori_loop(0, len(outs) * share // size, group, 0)
    for g in range(2):
        copies(g)[0].wait()


def first_kernel(count, blocks, shares, picks, got_ref, left, right, *refs):
    outs, (
        got, rows, keys, starts, weight, total, stage,
        got_sems, out_sems,
    ) = refs[:shares], refs[shares:]
    pairs = blocks * T
    sources = got_ref.shape[0]
    chunks = sources * count // T
    per = T // count
    batch = got.shape[1]
    rounds = sources // batch

    def arrival(r, buffer):
        return pltpu.make_async_copy(
            got_ref.at[pl.ds(r * batch, batch)], got.at[buffer], got_sems.at[buffer]
        )

    for r in range(ARRIVING):
        arrival(r, r).start()
    rows[chunks * T :, :] = jnp.zeros((FIRST * T, 2 * T), BF16)
    keys[pl.ds(chunks, 8), :] = jnp.full((8, T), -1, jnp.int32)

    lanes = lax.broadcasted_iota(jnp.int32, (1, T), 1)

    def fill(r, carry):
        buffer = lax.rem(r, ARRIVING)
        arrival(r, buffer).wait()
        here = got.at[buffer]
        for j in range(batch // per):
            s = r * (batch // per) + j
            x = here[j * per : (j + 1) * per, 0:count, :].reshape(T, T)
            hi = x.astype(BF16)
            at = pl.ds(pl.multiple_of(s * T, T), T)
            rows[at, 0:T] = hi
            rows[at, T:] = (x - hi.astype(F32)).astype(BF16)
            key = here[j * per, count : count + 1, :]
            for i in range(1, per):
                key = jnp.where(lanes >= i * count, here[j * per + i, count : count + 1, :], key)
            keys[pl.ds(s, 1), :] = key.astype(jnp.int32)
        spread = here[:, count + 1, :]
        for f in range(FREQS):
            for n in range(blocks):
                lane = f * blocks + n
                weight[f, pl.ds(pl.multiple_of(n * T + r * batch, batch), batch), :] = jnp.broadcast_to(
                    spread[:, lane : lane + 1], (batch, T)
                )

        @pl.when(r + ARRIVING < rounds)
        def _():
            arrival(r + ARRIVING, buffer).start()

        return carry

    lax.fori_loop(0, rounds, fill, 0)
    held = keys[0:chunks, :]
    for i in range(NAB + 1):
        starts[i] = jnp.sum((held < i * pairs).astype(jnp.int32))

    half = 2 * T
    wide = FIRST * T
    place = lax.broadcasted_iota(jnp.int32, (half, wide), 0)

    def put(a, n, value):
        at = slice(n * half, (n + 1) * half)

        row = jnp.minimum(a, NAB - 2)
        slot = jnp.maximum(a, 1) - 1
        turned = value.T
        hi = turned.astype(BF16)
        lo = (turned - hi.astype(F32)).astype(BF16)
        left[row, 0:T, at] = hi
        left[row, T:, at] = lo
        for f in range(FREQS):
            scaled = value * weight[f, at, :]
            hi = scaled.astype(BF16)
            cols = slice(f * T, (f + 1) * T)
            right[slot, 0, at, cols] = hi
            right[slot, 1, at, cols] = (scaled - hi.astype(F32)).astype(BF16)

    def straight(a):
        begin = starts[a]
        base = (begin // 16) * 16
        chunk = base // T
        near = jnp.concatenate([keys[pl.ds(chunk + j, 1), :] for j in range(FIRST + 1)], axis=1)
        near = jnp.broadcast_to(near, (8, wide + T))
        near = pltpu.roll(near, wide + T - (base - chunk * T), 1)
        key = near[0:1, 0:wide] - a * pairs
        source = rows[pl.ds(pl.multiple_of(base, 16), wide), :]
        for n in range(pairs // half):
            hot = jnp.where(place == key - n * half, 1.0, 0.0).astype(BF16)
            both = jnp.dot(hot, source, preferred_element_type=F32)
            put(a, n, both[:, 0:T] + both[:, T:])

    def whole(a):
        total[...] = jnp.zeros_like(total)

        def add(s, carry):
            key = keys[pl.ds(s, 1), :] - a * pairs
            for n in range(pairs // half):
                hot = jnp.where(place[:, 0:T] == key - n * half, 1.0, 0.0).astype(BF16)
                both = jnp.dot(hot, rows[pl.ds(pl.multiple_of(s * T, T), T), :], preferred_element_type=F32)
                total[n * half : (n + 1) * half, :] += both[:, 0:T] + both[:, T:]
            return carry

        lax.fori_loop(starts[a] // T, (starts[a + 1] + T - 1) // T, add, 0)
        for n in range(pairs // half):
            put(a, n, total[n * half : (n + 1) * half, :])

    def beyond(a):
        return starts[a + 1] - (starts[a] // 16) * 16 > wide

    def columns(i, carry):
        last = 2 * i == NAB - 2
        pair = jnp.where(last, NAB - 1, 2 * i), jnp.where(last, NAB - 2, 2 * i + 1)
        for a in pair:
            straight(a)

        @pl.when(jnp.logical_or(beyond(pair[0]), beyond(pair[1])))
        def _():
            for a in pair:
                whole(a)

        return carry

    lax.fori_loop(0, NAB // 2, columns, 0)
    multiply(0, picks, left, right, stage, outs, out_sems)


def first_products(picks, tiles, got, count, blocks):
    sources = got.shape[0]
    chunks = sources * count // T
    pairs = blocks * T
    shares = 2
    return pl.pallas_call(
        functools.partial(first_kernel, count, blocks, shares),
        grid_spec=pltpu.PrefetchScalarGridSpec(
            num_scalar_prefetch=1,
            grid=(),
            in_specs=[pl.BlockSpec(memory_space=pl.ANY)],
            out_specs=[pl.BlockSpec(memory_space=pltpu.VMEM)] * 2 + [pl.BlockSpec(memory_space=pl.ANY)] * shares,
            scratch_shapes=[
                pltpu.VMEM((ARRIVING, BATCH) + got.shape[1:], F32),
                pltpu.VMEM(((chunks + FIRST) * T, 2 * T), BF16),
                pltpu.VMEM((chunks + 8, T), jnp.int32),
                pltpu.SMEM((NAB + 1,), jnp.int32),
                pltpu.VMEM((FREQS, pairs, T), F32),
                pltpu.VMEM((pairs, T), F32),
                pltpu.VMEM((2, GROUP, FREQS, T, T), F32),
                pltpu.SemaphoreType.DMA((ARRIVING,)),
                pltpu.SemaphoreType.DMA((2,)),
            ],
        ),
        out_shape=[
            pltpu.VMEM((NAB - 1, 2 * T, pairs), BF16),
            pltpu.VMEM((NAB - 1, 2, pairs, FREQS * T), BF16),
        ]
        + [pltpu.HBM((tiles // shares, FREQS, T, T), F32)] * shares,
        compiler_params=pltpu.CompilerParams(vmem_limit_bytes=KERNEL_MIB * MIB),
        name="first_products",
    )(picks, got)


def more_kernel(at, fences, picks, left, right, *refs):
    outs, (stage, out_sems) = refs[fences:-2], refs[-2:]
    multiply(at, picks, left, right, stage, outs, out_sems)


def more_products(at, picks, left, right, fence=()):
    return pl.pallas_call(
        functools.partial(more_kernel, at, len(fence)),
        grid_spec=pltpu.PrefetchScalarGridSpec(
            num_scalar_prefetch=1,
            grid=(),
            in_specs=[pl.BlockSpec(memory_space=pltpu.VMEM)] * 2
            + [pl.BlockSpec(memory_space=pl.ANY)] * len(fence),
            out_specs=[pl.BlockSpec(memory_space=pl.ANY)] * 2,
            scratch_shapes=[
                pltpu.VMEM((2, 16, FREQS, T, T), F32),
                pltpu.SemaphoreType.DMA((2,)),
            ],
        ),
        out_shape=[pltpu.HBM((16, FREQS, T, T), F32)] * 2,
        compiler_params=pltpu.CompilerParams(vmem_limit_bytes=KERNEL_MIB * MIB),
        cost_estimate=pl.CostEstimate(
            flops=12 * GROUP * FREQS * T * T * left.shape[2], bytes_accessed=4 * MIB, transcendentals=0
        ),
        name="more_products",
    )(
        picks,
        pltpu.with_memory_space_constraint(left, pltpu.VMEM),
        pltpu.with_memory_space_constraint(right, pltpu.VMEM),
        *fence,
    )


def add_kernel(a_low, a_high, b_low, b_high, low, high):
    low[...] = a_low[...] + b_low[...]
    high[...] = a_high[...] + b_high[...]


def add_halves(a, b):
    half = a.shape[0] // 2
    step = 4
    a = pltpu.with_memory_space_constraint(a, pltpu.HBM)
    b = pltpu.with_memory_space_constraint(b, pltpu.HBM)
    block = (step,) + a.shape[1:]
    first = pl.BlockSpec(block, lambda i: (i, 0, 0, 0))
    second = pl.BlockSpec(block, lambda i: (i + half // step, 0, 0, 0))
    return pl.pallas_call(
        add_kernel,
        grid=(half // step,),
        in_specs=[first, second, first, second],
        out_specs=[first, first],
        out_shape=[pltpu.HBM((half,) + a.shape[1:], F32)] * 2,
        compiler_params=pltpu.CompilerParams(vmem_limit_bytes=KERNEL_MIB * MIB),
        name="add_halves",
    )(a, a, b, b)


def layout(me, owner):
    plane = jnp.arange(16, dtype=jnp.int32)
    high, low = plane // 4, plane % 4
    here = jnp.where(owner == 0, me % 4, me // 32)
    lists = []
    for step in (2, 1, 3, 0):
        at = (here + step) % 4
        lists.append(
            jnp.where(owner == 0, ((high * 4 + low) * 2) * 4 + at, ((at * 4 + high) * 2 + 1) * 4 + low)
        )
    return lists


def shift(step):
    pairs = []
    for d in range(128):
        x, y, core, z = d // 32, d // 8 % 4, d // 4 % 2, d % 4
        if core == 0:
            z = (z + step) % 4
        else:
            x = (x + step) % 4
        pairs.append((d, ((x * 4 + y) * 2 + core) * 4 + z))
    return pairs


PLANES = [[(plane * 2) * 4 + z for plane in range(16)] for z in range(4)] + [
    [((x * 4 + plane // 4) * 2 + 1) * 4 + plane % 4 for plane in range(16)] for x in range(4)
]
SWAP = [(d, d ^ 4) for d in range(128)]


def on_device(b_tiles, tile_aux, tile_pair, freq_weights, kept):
    count = b_tiles.shape[0]
    devices = lax.axis_size("d")
    me = lax.axis_index("d")
    core = me // 4 % 2
    blocks = freq_weights.shape[1] // T

    sent = by_column(b_tiles, tile_aux, tile_pair, freq_weights, devices).reshape(devices, count + EXTRA, T)
    got = lax.all_to_all(sent, "d", split_axis=0, concat_axis=0, tiled=True)

    far, up, down, keep = zip(*[layout(me, owner) for owner in (1 - core, core)])
    low, high = slice(0, 8), slice(8, 16)
    lists = [
        [far[0], far[1]],
        [up[0][high], down[0][low], up[1][high], down[1][low]],
        [up[0][low], down[0][high], up[1][low], down[1][high]],
        [keep[0], keep[1]],
    ]
    picks = kept[jnp.concatenate([part for some in lists for part in some])].reshape(-1)

    def swap(tiles):
        return lax.ppermute(tiles, "d", SWAP)

    def send(pair):
        return [lax.ppermute(part, "d", shift(step)) for part, step in zip(pair, (1, -1))]

    left, right, away, far = first_products(picks, 32, got, count, blocks)
    landed = swap(away)
    away, second = more_products(32, picks, left, right)
    away, landed = lax.optimization_barrier((away, landed))

    leaving = add_halves(far, landed)
    passing = send(leaving)
    landed = swap(away)
    away, third = more_products(64, picks, left, right, leaving)
    away, landed, passing = lax.optimization_barrier((away, landed, passing))

    leaving = add_halves(second, landed)
    arrived = send(leaving)
    landed = swap(away)
    away, keep = more_products(96, picks, left, right, leaving)
    away, landed, arrived = lax.optimization_barrier((away, landed, arrived))

    last = send([third[low] + landed[low] + passing[0], third[high] + landed[high] + passing[1]])
    landed = swap(away)
    summed = jnp.concatenate(
        [
            keep[low] + landed[low] + last[0] + arrived[1],
            keep[high] + landed[high] + last[1] + arrived[0],
        ]
    )
    parts = lax.all_to_all(summed, "d", split_axis=0, concat_axis=0, tiled=True, axis_index_groups=PLANES)
    return jnp.sum(parts, axis=0, keepdims=True)


def solution(mesh):
    flat = Mesh(mesh.devices.reshape(-1), ("d",))
    placed = (P("d", None, None), P("d"), P("d"), P(None, "d"), P())
    return jax.shard_map(
        on_device, mesh=flat, in_specs=placed, out_specs=P("d", None, None, None), check_vma=False
    )
```
